32 devices in a mesh: grp: 2 (over y), row: 4 (over x, core), col: 4 (over z).
Axes of the slice: x: 2, y: 2, z: 4, core: 2. Of those that a mesh axis runs over, the one named last changes fastest.
Arguments:
- root_inverse: float32 [4096, 2048], P(('grp', 'row'), 'col'), parts along dimension 0, may hold values from -1 to 4, as said below
- panel: float32 [4096, 2048], P(('grp', 'row'), 'col'), parts along dimension 0, may hold values from -0.125 to 0.125
- node_inverse: float32 [4096, 2048], P(('grp', 'row'), 'col'), parts along dimension 0, may hold values from -1 to 4, as said below
- structure: int32 [64], P(('grp', 'row')), parts along dimension 0, may hold values 0 or 1
Outputs:
- sigma_root: float32 [4096, 2048], P(('grp', 'row'), 'col'), parts along dimension 0
- sigma_off: float32 [4096, 2048], P(('grp', 'row'), 'col'), parts along dimension 0
- sigma_node: float32 [4096, 2048], P(('grp', 'row'), 'col'), parts along dimension 0
The draws below stay inside these ranges and needn't reach their ends.
There are 2 independent parts, one for each index of `grp`. The reference program is written for one: setup_inputs(seed, part) draws one part's arguments, and reference() takes and returns one part's arrays. A program takes and returns all parts, laid end to end along the dimension named above; each array names one. Nothing has to cross between parts.
Inputs may be any that keep to these rules, and one draw needn't show every extreme that they name: `root_inverse`: lower triangular, diagonal entries 1 or more. `node_inverse`: lower triangular, diagonal entries 1 or more.
All inputs are finite; a program needn't handle non-finite values. No bound on the sum of `structure` on one device may be relied on, other than what follows from the above.
Results may differ from the reference program's by a relative error of at most 0.000098.
Values sent between devices are 32-bit elements; how exact they have to be, the bound alone decides.
A program may use at most 128 MiB of HBM per device.

```python
import math
import jax
import jax.numpy as jnp
from jax import lax

NA = 2048
NB = 2048
BS = 64
BLOCKS = 32


def assemble(off_values, diag_values):
    matrix_order = diag_values.shape[0]
    index_list = jnp.arange(matrix_order)
    beneath = index_list[:, None] > index_list[None, :]
    return jnp.where(beneath, off_values, 0.0) + jnp.diag(diag_values)


def draw_root_inverse(key, part):
    key = jax.random.fold_in(key, 11)
    off_key, diag_key = jax.random.split(key)
    spread = 0.6 / math.sqrt(NA)
    off_values = spread * jax.random.normal(off_key, (NA, NA), jnp.float32)
    diag_values = jax.random.uniform(diag_key, (NA,), jnp.float32, 1.0, 2.0)
    return assemble(off_values, diag_values)


def draw_node_inverse(key, part):
    key = jax.random.fold_in(key, 23)
    off_key, diag_key = jax.random.split(key)
    spread = 0.6 / math.sqrt(NB)
    off_values = spread * jax.random.normal(off_key, (NB, NB), jnp.float32)
    diag_values = jax.random.uniform(diag_key, (NB,), jnp.float32, 1.0, 2.0)
    return assemble(off_values, diag_values)


def with_ends(drawn, own_key, low, high):
    shape = drawn.shape
    place = [jax.random.randint(jax.random.fold_in(own_key, axis), (), 0, shape[axis]) for axis in range(len(shape))]
    drawn = drawn.at[tuple(place)].set(low)
    longest = shape.index(max(shape))
    place[longest] = (place[longest] + 1) % shape[longest]
    return drawn.at[tuple(place)].set(high)


def steps_of(rng, extent, cuts, least, largest):
    factor_of = 1.0
    for axis_at, blocks in cuts:
        steps = jax.random.uniform(jax.random.fold_in(jax.random.fold_in(rng, 6), axis_at), (blocks,), jnp.float32, least / len(cuts), largest / len(cuts))
        factor_of = factor_of * jnp.repeat(jnp.exp(steps), extent[axis_at] // blocks).reshape((-1,) + (1,) * (len(extent) - 1 - axis_at))
    return factor_of


def scatter_about(stream_key, dims, width, limit, shards=(), kind=jnp.bfloat16):
    values = jax.random.normal(stream_key, dims, jnp.float32) * width
    if len(shards) > 0:
        values = steps_of(stream_key, dims, shards, -0.22, 0.18) * values
    return jnp.clip(values, min=-limit, max=limit).astype(kind)


def setup_inputs(seed: int = 0, part: int = 0) -> dict:
    streams_of = jax.random.split(jax.random.key(seed), 5)
    part_keys = jax.random.split(jax.random.fold_in(streams_of[4], part), 5)
    root_inverse = draw_root_inverse(jax.random.fold_in(jax.random.fold_in(streams_of[4], part), 71), part)
    panel = scatter_about(part_keys[1], (NA, NB), NA ** -0.5, 0.125, ((0, 4), (1, 4)), jnp.float32)
    node_inverse = draw_node_inverse(jax.random.fold_in(jax.random.fold_in(streams_of[4], part), 71), part)
    structure = with_ends((jax.random.randint(part_keys[3], (BLOCKS,), 0, 4) < 3).astype(jnp.int32), jax.random.fold_in(part_keys[3], 1), 0, 1)
    return dict(root_inverse=root_inverse, panel=panel, node_inverse=node_inverse, structure=structure)


PRECISE = lax.Precision.HIGHEST


def product(left_side, right_side):
    return jnp.dot(left_side, right_side, precision=PRECISE, preferred_element_type=jnp.float32)


def reference(root_inverse, panel, node_inverse, structure):
    sigma_root = product(root_inverse.T, root_inverse)
    row_mask = jnp.repeat(structure, BS).astype(jnp.float32)
    masked = panel * row_mask[:, None]
    scaled = product(masked, node_inverse)
    sigma_off = -product(sigma_root, scaled)
    sigma_node = product(node_inverse.T, node_inverse) - product(scaled.T, sigma_off)
    return sigma_root, sigma_off, sigma_node
```

```python
import functools

import jax
import jax.numpy as jnp
from jax import lax
from jax.experimental import pallas as pl
from jax.experimental.pallas import tpu as pltpu
from jax.sharding import PartitionSpec as P

BS = 64
MESH = pl.DeviceIdType.MESH
F32, BF16 = jnp.float32, jnp.bfloat16


def halves(v):
    high = v.astype(BF16)
    return high, (v - high.astype(F32)).astype(BF16)


def multiply(dst, a, b, transposed, add):
    order = dst.shape[1]
    tile = min(256, order)
    dims = (((0 if transposed else 1,), (0,)), ((), ()))

    def dot(u, v):
        return lax.dot_general(u, v, dims, preferred_element_type=F32)

    def body(t, carry):
        cols = pl.ds(pl.multiple_of(t * tile, tile), tile)
        ah, al = halves(a[...])
        bh, bl = halves(b[:, cols])
        r = dot(ah, bh) + (dot(ah, bl) + dot(al, bh))
        if add:
            r = dst[:, cols] + r
        dst[:, cols] = r
        return carry

    lax.fori_loop(0, order // tile, body, 0)


def kernel(R, C, root, panel, node, mask, out_rr, out_or, out_nn,
           Mb, Rb, Nr, Nc, Xc, Yb, S, A, T1, T2,
           m_s, m_r, r_s, r_r, n_s, n_r, y_s, y_r,
           c_x, c_p, c_r, x_x, x_p, x_r, s1, q1, s2, q2):
    X = R // 2
    i, j = lax.axis_index("row"), lax.axis_index("col")
    x, c = i // 2, lax.rem(i, 2)
    mate = 2 * x + 1 - c
    left, right = lax.rem(j + C - 1, C), lax.rem(j + 1, C)
    k = R - 1 - i

    def copy(src, dst, ssem, rsem, row=None, col=None):
        device = {"row": i if row is None else row, "col": j if col is None else col}
        return pltpu.make_async_remote_copy(
            src_ref=src, dst_ref=dst, send_sem=ssem, recv_sem=rsem,
            device_id=device, device_id_type=MESH)

    def loop(low, high, body):
        def step(t, carry):
            body(t)
            return carry
        lax.fori_loop(low, high, step, 0)

    def when(*conditions):
        both = conditions[0]
        for condition in conditions[1:]:
            both = jnp.logical_and(both, condition)
        return pl.when(both)

    barrier = pltpu.get_barrier_semaphore()

    def greet(row, col):
        pl.semaphore_signal(barrier, inc=1, device_id={"row": row, "col": col}, device_id_type=MESH)

    @pl.when(j > 0)
    def _():
        greet(i, j - 1)

    @pl.when(j < C - 1)
    def _():
        greet(i, j + 1)

    greet(mate, j)
    loop(1, X, lambda d: greet(2 * lax.rem(x + d, X) + c, j))
    pl.semaphore_wait(barrier, X + jnp.where(j > 0, 1, 0) + jnp.where(j < C - 1, 1, 0))

    def to_left(buf, sends, arrivals, l):
        return copy(buf.at[l], buf.at[l], sends.at[0, l], arrivals.at[l], col=left)

    def to_right(buf, sends, arrivals, l):
        return copy(buf.at[l], buf.at[l], sends.at[1, l], arrivals.at[l], col=right)

    def pass_on(buf, sends, arrivals, r, top, end, go_right):
        l = j + r

        @when(l <= top, l < C, j <= end)
        def _():
            if not (isinstance(r, int) and r == 0):
                to_left(buf, sends, arrivals, l).wait_recv()

            @pl.when(j > 0)
            def _():
                to_left(buf, sends, arrivals, l).start()

        if go_right:
            m = j - r

            @when(m >= 0, m <= top, j <= end)
            def _():
                if not (isinstance(r, int) and r == 0):
                    to_left(buf, sends, arrivals, m).wait_recv()

                @when(j < C - 1, j < end)
                def _():
                    to_right(buf, sends, arrivals, m).start()

    def sent_on(buf, sends, arrivals, top, end, go_right):
        def body(r):
            l, m = j + r, j - r

            @when(l <= top, l < C, j <= end, j > 0)
            def _():
                to_left(buf, sends, arrivals, l).wait_send()

            if go_right:
                @when(m >= 0, m <= top, j <= end, j < C - 1, j < end)
                def _():
                    to_right(buf, sends, arrivals, m).wait_send()
        loop(0, C, body)

    def across(buf, sems, arrivals, d_chip):
        return copy(buf.at[i], buf.at[i], sems.at[d_chip], arrivals.at[i], row=2 * d_chip + c)

    def over(buf, sems, arrivals, l):
        return copy(buf.at[l], buf.at[l], sems.at[l], arrivals.at[l], row=mate)

    def spread(buf, xs, ps, arrivals, cross, own):
        def body(d):
            chip = lax.rem(x + d, X)

            @pl.when(cross(i, x, chip))
            def _():
                across(buf, xs, arrivals, chip).start()
        loop(1, X, body)

        @pl.when(own(i))
        def _():
            over(buf, ps, arrivals, i).start()

    def collect(buf, xs, ps, arrivals, cross, own):
        def body(d):
            chip = lax.rem(x + X - d, X)
            l = 2 * chip + c

            @pl.when(cross(l, chip, x))
            def _():
                over(buf, ps, arrivals, l).wait_recv()
                over(buf, ps, arrivals, l).start()
        loop(1, X, body)

        def rest(d):
            chip = lax.rem(x + X - d, X)
            l = 2 * chip + 1 - c

            @pl.when(jnp.where(chip == x, own(l), cross(l, chip, x)))
            def _():
                over(buf, ps, arrivals, l).wait_recv()
        loop(0, X, rest)

    def spread_done(buf, xs, ps, arrivals, cross, own):
        def body(d):
            chip = lax.rem(x + d, X)

            @pl.when(cross(i, x, chip))
            def _():
                across(buf, xs, arrivals, chip).wait_send()
            source = lax.rem(x + X - d, X)
            l = 2 * source + c

            @pl.when(cross(l, source, x))
            def _():
                over(buf, ps, arrivals, l).wait_send()
        loop(1, X, body)

        @pl.when(own(i))
        def _():
            over(buf, ps, arrivals, i).wait_send()

    def core_copy(n, chip):
        return copy(S.at[chip], T1.at[n, chip], s1.at[chip], q1.at[n, chip], row=mate)

    def chip_copy(n, chip, slot):
        return copy(A.at[chip], T2.at[n, slot], s2.at[chip], q2.at[n, slot], row=2 * chip + c)

    def sum_first(n, partial, into):
        def body(d):
            chip = lax.rem(x + d, X)

            @pl.when(into(x, chip))
            def _():
                partial(S.at[chip], 2 * chip + 1 - c)
                core_copy(n, chip).start()
                partial(A.at[chip], 2 * chip + c)
        loop(1, X + 1, body)

    def sum_second(n, into):
        def body(d):
            chip = lax.rem(x + d, X)

            @pl.when(into(x, chip))
            def _():
                core_copy(n, chip).wait_recv()
                A[chip] = A[chip] + T1[n, chip]

                @pl.when(chip != x)
                def _():
                    chip_copy(n, chip, x).start()
        loop(1, X + 1, body)

    def sum_last(n, out, into, sign):
        total = A.at[x]

        def body(d):
            chip = lax.rem(x + d, X)

            @pl.when(into(chip, x))
            def _():
                chip_copy(n, chip, chip).wait_recv()
                total[...] = total[...] + T2[n, chip]
        loop(1, X, body)
        out[...] = total[...] if sign > 0 else 0.0 - total[...]

        def sent(d):
            chip = lax.rem(x + d, X)

            @pl.when(into(x, chip))
            def _():
                core_copy(n, chip).wait_send()

                @pl.when(chip != x)
                def _():
                    chip_copy(n, chip, x).wait_send()
        loop(1, X + 1, sent)

    every = C - 1
    M_line = (Mb, m_s, m_r)
    R_line = (Rb, r_s, r_r)
    N_line = (Nr, n_s, n_r)
    Y_line = (Yb, y_s, y_r)
    N_col = (Nc, c_x, c_p, c_r, lambda l, a, b: l >= j, lambda l: l >= j)
    X_col = (Xc, x_x, x_p, x_r, lambda l, a, b: a < b, lambda l: lax.rem(l, 2) == 0)

    Mb[j] = panel[...] * mask[...]
    pass_on(*M_line, 0, every, every, False)
    Nc[i] = node[...]
    spread(*N_col)

    @when(c == 0, j != i + 1)
    def _():
        Rb[i + 1] = jnp.zeros(root.shape, F32)
    Rb[j] = root[...]
    pass_on(*R_line, 0, i, every, True)
    collect(*N_col)

    @pl.when(j <= k)
    def _():
        Nr[j] = Nc[k]
    pass_on(*N_line, 0, k, k, True)

    multiply(Xc.at[i], Mb.at[j], Nc.at[j], False, False)

    def arrive(r):
        pass_on(*M_line, r, every, every, False)
        pass_on(*R_line, r, i, every, True)
        pass_on(*N_line, r, k, k, True)

        @pl.when(j + r < C)
        def _():
            multiply(Xc.at[i], Mb.at[j + r], Nc.at[j + r], False, True)
    loop(1, C, arrive)
    spread(*X_col)

    below = lambda a, b: b <= a
    sum_first(0, lambda dst, t: multiply(dst, Rb.at[t], Rb.at[j], True, False), below)
    sum_second(0, below)
    collect(*X_col)

    multiply(Yb.at[j], Rb.at[0], Xc.at[0], False, False)
    loop(1, i + 1, lambda t: multiply(Yb.at[j], Rb.at[t], Xc.at[t], False, True))
    pass_on(*Y_line, 0, every, every, True)
    sum_last(0, out_rr, below, 1)

    sum_first(1, lambda dst, t: multiply(dst, Rb.at[t], Yb.at[j], True, False), below)
    sum_second(1, below)
    loop(1, C, lambda r: pass_on(*Y_line, r, every, every, True))
    sum_last(1, out_or, below, -1)

    def node_part(dst, t):
        multiply(dst, Yb.at[t], Yb.at[j], True, False)

        @when(t <= k, j <= k)
        def _():
            multiply(dst, Nr.at[t], Nr.at[j], True, True)
    always = lambda a, b: a >= 0
    sum_first(2, node_part, always)
    sum_second(2, always)
    sum_last(2, out_nn, always, 1)

    sent_on(*M_line, every, every, False)
    sent_on(*R_line, i, every, True)
    sent_on(*N_line, k, k, True)
    sent_on(*Y_line, every, every, True)
    spread_done(*N_col)
    spread_done(*X_col)


def shards(R, C, root_inverse, panel, node_inverse, structure):
    B = root_inverse.shape[0]
    X = R // 2
    mask = jnp.repeat(structure, BS).astype(F32)[:, None]
    block = jax.ShapeDtypeStruct((B, B), F32)
    dma = pltpu.SemaphoreType.DMA
    slots = lambda *n: pltpu.VMEM(n + (B, B), F32)
    vmem = pl.BlockSpec(memory_space=pltpu.VMEM)
    return pl.pallas_call(
        functools.partial(kernel, R, C),
        out_shape=(block, block, block),
        in_specs=[vmem] * 4,
        out_specs=(vmem,) * 3,
        scratch_shapes=[
            slots(C), slots(C), slots(C), slots(R), slots(R), slots(C),
            slots(X), slots(X), slots(3, X), slots(3, X),
        ] + [dma((2, C)), dma((C,))] * 4 + [dma((X,)), dma((R,)), dma((R,))] * 2 + [
            dma((X,)), dma((3, X)), dma((X,)), dma((3, X)),
        ],
        compiler_params=pltpu.CompilerParams(
            collective_id=0, has_side_effects=True, vmem_limit_bytes=60 * 2**20),
    )(root_inverse, panel, node_inverse, mask)


def solution(mesh):
    placed = (
        P(("grp", "row"), "col"),
        P(("grp", "row"), "col"),
        P(("grp", "row"), "col"),
        P(("grp", "row")),
    )
    return jax.shard_map(
        functools.partial(shards, mesh.shape["row"], mesh.shape["col"]),
        mesh=mesh,
        in_specs=placed,
        out_specs=(P(("grp", "row"), "col"), P(("grp", "row"), "col"), P(("grp", "row"), "col")),
        check_vma=False,
    )
```

```python
import functools

import jax
import jax.numpy as jnp
from jax import lax
from jax.experimental import pallas as pl
from jax.experimental.pallas import tpu as pltpu
from jax.sharding import PartitionSpec as P

BS = 64
MESH = pl.DeviceIdType.MESH
F32, BF16 = jnp.float32, jnp.bfloat16


def halves(v):
    high = v.astype(BF16)
    return high, (v - high.astype(F32)).astype(BF16)


def multiply(dst, a, b, transposed, add):
    order = dst.shape[1]
    tile = min(256, order)
    dims = (((0 if transposed else 1,), (0,)), ((), ()))

    def dot(u, v):
        return lax.dot_general(u, v, dims, preferred_element_type=F32)

    def body(t, carry):
        cols = pl.ds(pl.multiple_of(t * tile, tile), tile)
        ah, al = halves(a[...])
        bh, bl = halves(b[:, cols])
        r = dot(ah, bh) + (dot(ah, bl) + dot(al, bh))
        if add:
            r = dst[:, cols] + r
        dst[:, cols] = r
        return carry

    lax.fori_loop(0, order // tile, body, 0)


def kernel(R, C, root, panel, node, mask, out_rr, out_or, out_nn,
           Mb, Rb, Nr, Nc, N0, X0, Xc, Yb, S, A, T1, T2,
           m_s, m_r, r_s, r_r, n_s, n_r, y_s, y_r,
           c_x, c_p, c_r, d_x, d_p, d_r, x_x, x_p, x_r, s1, q1, s2, q2, h_s, h_r):
    X = R // 2
    i, j = lax.axis_index("row"), lax.axis_index("col")
    x, c = i // 2, lax.rem(i, 2)
    mate = 2 * x + 1 - c
    left, right = lax.rem(j + C - 1, C), lax.rem(j + 1, C)
    k = R - 1 - i

    def copy(src, dst, ssem, rsem, row=None, col=None):
        device = {"row": i if row is None else row, "col": j if col is None else col}
        return pltpu.make_async_remote_copy(
            src_ref=src, dst_ref=dst, send_sem=ssem, recv_sem=rsem,
            device_id=device, device_id_type=MESH)

    def loop(low, high, body):
        def step(t, carry):
            body(t)
            return carry
        lax.fori_loop(low, high, step, 0)

    def when(*conditions):
        both = conditions[0]
        for condition in conditions[1:]:
            both = jnp.logical_and(both, condition)
        return pl.when(both)

    barrier = pltpu.get_barrier_semaphore()

    def greet(row, col):
        pl.semaphore_signal(barrier, inc=1, device_id={"row": row, "col": col}, device_id_type=MESH)

    @pl.when(j > 0)
    def _():
        greet(i, j - 1)

    @pl.when(j < C - 1)
    def _():
        greet(i, j + 1)

    greet(mate, j)
    loop(1, X, lambda d: greet(2 * lax.rem(x + d, X) + c, j))
    pl.semaphore_wait(barrier, X + jnp.where(j > 0, 1, 0) + jnp.where(j < C - 1, 1, 0))

    def to_left(buf, sends, arrivals, l):
        return copy(buf.at[l], buf.at[l], sends.at[0, l], arrivals.at[l], col=left)

    def to_right(buf, sends, arrivals, l):
        return copy(buf.at[l], buf.at[l], sends.at[1, l], arrivals.at[l], col=right)

    def pass_on(buf, sends, arrivals, r, top, end, go_right, low=0):
        l = j + r

        @when(l <= top, l < C, j <= end, j >= low)
        def _():
            if not (isinstance(r, int) and r == 0):
                to_left(buf, sends, arrivals, l).wait_recv()

            @pl.when(j > low)
            def _():
                to_left(buf, sends, arrivals, l).start()

        if go_right:
            m = j - r

            @when(m >= 0, m <= top, j <= end)
            def _():
                if not (isinstance(r, int) and r == 0):
                    to_left(buf, sends, arrivals, m).wait_recv()

                @when(j < C - 1, j < end)
                def _():
                    to_right(buf, sends, arrivals, m).start()

    def sent_on(buf, sends, arrivals, top, end, go_right, low=0):
        def body(r):
            l, m = j + r, j - r

            @when(l <= top, l < C, j <= end, j > low)
            def _():
                to_left(buf, sends, arrivals, l).wait_send()

            if go_right:
                @when(m >= 0, m <= top, j <= end, j < C - 1, j < end)
                def _():
                    to_right(buf, sends, arrivals, m).wait_send()
        loop(0, C, body)

    def across(buf, sems, arrivals, d_chip):
        return copy(buf.at[i], buf.at[i], sems.at[d_chip], arrivals.at[i], row=2 * d_chip + c)

    def over(buf, sems, arrivals, l):
        return copy(buf.at[l], buf.at[l], sems.at[l], arrivals.at[l], row=mate)

    def spread(buf, xs, ps, arrivals, cross, own):
        def body(d):
            chip = lax.rem(x + d, X)

            @pl.when(cross(i, x, chip))
            def _():
                across(buf, xs, arrivals, chip).start()
        loop(1, X, body)

        @pl.when(own(i))
        def _():
            over(buf, ps, arrivals, i).start()

    def collect(buf, xs, ps, arrivals, cross, own):
        def body(d):
            chip = lax.rem(x + X - d, X)
            l = 2 * chip + c

            @pl.when(cross(l, chip, x))
            def _():
                over(buf, ps, arrivals, l).wait_recv()
                over(buf, ps, arrivals, l).start()
        loop(1, X, body)

        def rest(d):
            chip = lax.rem(x + X - d, X)
            l = 2 * chip + 1 - c

            @pl.when(jnp.where(chip == x, own(l), cross(l, chip, x)))
            def _():
                over(buf, ps, arrivals, l).wait_recv()
        loop(0, X, rest)

    def spread_done(buf, xs, ps, arrivals, cross, own):
        def body(d):
            chip = lax.rem(x + d, X)

            @pl.when(cross(i, x, chip))
            def _():
                across(buf, xs, arrivals, chip).wait_send()
            source = lax.rem(x + X - d, X)
            l = 2 * source + c

            @pl.when(cross(l, source, x))
            def _():
                over(buf, ps, arrivals, l).wait_send()
        loop(1, X, body)

        @pl.when(own(i))
        def _():
            over(buf, ps, arrivals, i).wait_send()

    def core_copy(n, chip):
        return copy(S.at[chip], T1.at[n, chip], s1.at[chip], q1.at[n, chip], row=mate)

    def chip_copy(n, chip, slot):
        return copy(A.at[chip], T2.at[n, slot], s2.at[chip], q2.at[n, slot], row=2 * chip + c)

    def sum_first(n, partial, into):
        def body(d):
            chip = lax.rem(x + d, X)

            @pl.when(into(x, chip))
            def _():
                partial(S.at[chip], 2 * chip + 1 - c)
                core_copy(n, chip).start()
                partial(A.at[chip], 2 * chip + c)
        loop(1, X + 1, body)

    def sum_second(n, into):
        def body(d):
            chip = lax.rem(x + d, X)

            @pl.when(into(x, chip))
            def _():
                core_copy(n, chip).wait_recv()
                A[chip] = A[chip] + T1[n, chip]

                @pl.when(chip != x)
                def _():
                    chip_copy(n, chip, x).start()
        loop(1, X + 1, body)

    def sum_last(n, out, into, sign):
        total = A.at[x]

        def body(d):
            chip = lax.rem(x + d, X)

            @pl.when(into(chip, x))
            def _():
                chip_copy(n, chip, chip).wait_recv()
                total[...] = total[...] + T2[n, chip]
        loop(1, X, body)
        out[...] = total[...] if sign > 0 else 0.0 - total[...]

        def sent(d):
            chip = lax.rem(x + d, X)

            @pl.when(into(x, chip))
            def _():
                core_copy(n, chip).wait_send()

                @pl.when(chip != x)
                def _():
                    chip_copy(n, chip, x).wait_send()
        loop(1, X + 1, sent)

    every = C - 1
    M_line = (Mb, m_s, m_r)
    R_line = (Rb, r_s, r_r)
    N_line = (Nr, n_s, n_r)
    Y_line = (Yb, y_s, y_r)
    N_col = (Nc, c_x, c_p, c_r, lambda l, a, b: l >= j, lambda l: l >= j)
    N0_col = (N0, d_x, d_p, d_r, lambda l, a, b: l >= 0, lambda l: l >= 0)
    X_col = (Xc, x_x, x_p, x_r, lambda l, a, b: a < b, lambda l: lax.rem(l, 2) == 0)

    def node_hop():
        return copy(Nc.at[i], N0.at[i], h_s.at[0], h_r.at[0], col=right)

    def panel_hop():
        return copy(Mb.at[0], Mb.at[0], h_s.at[1], h_r.at[1], col=right)

    def scaled_hop():
        return copy(X0, Xc.at[i], h_s.at[2], h_r.at[2], col=left)

    Nc[i] = node[...]
    spread(*N_col)

    @pl.when(j == 0)
    def _():
        node_hop().start()
    Mb[j] = panel[...] * mask[...]

    @pl.when(j == 0)
    def _():
        panel_hop().start()
    pass_on(*M_line, 0, every, every, False, 1)

    @when(c == 0, j != i + 1)
    def _():
        Rb[i + 1] = jnp.zeros(root.shape, F32)
    Rb[j] = root[...]
    pass_on(*R_line, 0, i, every, True)

    @pl.when(j == 1)
    def _():
        node_hop().wait_recv()
        spread(*N0_col)
    collect(*N_col)

    @pl.when(j <= k)
    def _():
        Nr[j] = Nc[k]
    pass_on(*N_line, 0, k, k, True)

    @pl.when(j == 1)
    def _():
        collect(*N0_col)
        panel_hop().wait_recv()
        multiply(X0, Mb.at[0], N0.at[0], False, False)
        multiply(X0, Mb.at[1], N0.at[1], False, True)

    @pl.when(j > 0)
    def _():
        multiply(Xc.at[i], Mb.at[j], Nc.at[j], False, False)

    def arrive(r):
        pass_on(*M_line, r, every, every, False, 1)

        @when(j == 1, j + r < C)
        def _():
            multiply(X0, Mb.at[j + r], N0.at[j + r], False, True)

            @pl.when(j + r == C - 1)
            def _():
                scaled_hop().start()
        pass_on(*R_line, r, i, every, True)
        pass_on(*N_line, r, k, k, True)

        @when(j > 0, j + r < C)
        def _():
            multiply(Xc.at[i], Mb.at[j + r], Nc.at[j + r], False, True)
    loop(1, C, arrive)

    @pl.when(j == 0)
    def _():
        scaled_hop().wait_recv()
    spread(*X_col)

    below = lambda a, b: b <= a
    sum_first(0, lambda dst, t: multiply(dst, Rb.at[t], Rb.at[j], True, False), below)
    sum_second(0, below)
    collect(*X_col)

    multiply(Yb.at[j], Rb.at[0], Xc.at[0], False, False)
    loop(1, i + 1, lambda t: multiply(Yb.at[j], Rb.at[t], Xc.at[t], False, True))
    pass_on(*Y_line, 0, every, every, True)
    sum_last(0, out_rr, below, 1)

    sum_first(1, lambda dst, t: multiply(dst, Rb.at[t], Yb.at[j], True, False), below)
    sum_second(1, below)
    loop(1, C, lambda r: pass_on(*Y_line, r, every, every, True))
    sum_last(1, out_or, below, -1)

    def node_part(dst, t):
        multiply(dst, Yb.at[t], Yb.at[j], True, False)

        @when(t <= k, j <= k)
        def _():
            multiply(dst, Nr.at[t], Nr.at[j], True, True)
    always = lambda a, b: a >= 0
    sum_first(2, node_part, always)
    sum_second(2, always)
    sum_last(2, out_nn, always, 1)

    sent_on(*M_line, every, every, False, 1)

    @pl.when(j == 0)
    def _():
        node_hop().wait_send()
        panel_hop().wait_send()

    @pl.when(j == 1)
    def _():
        scaled_hop().wait_send()
        spread_done(*N0_col)
    sent_on(*R_line, i, every, True)
    sent_on(*N_line, k, k, True)
    sent_on(*Y_line, every, every, True)
    spread_done(*N_col)
    spread_done(*X_col)


def shards(R, C, root_inverse, panel, node_inverse, structure):
    B = root_inverse.shape[0]
    X = R // 2
    mask = jnp.repeat(structure, BS).astype(F32)[:, None]
    block = jax.ShapeDtypeStruct((B, B), F32)
    dma = pltpu.SemaphoreType.DMA
    slots = lambda *n: pltpu.VMEM(n + (B, B), F32)
    vmem = pl.BlockSpec(memory_space=pltpu.VMEM)
    return pl.pallas_call(
        functools.partial(kernel, R, C),
        out_shape=(block, block, block),
        in_specs=[vmem] * 4,
        out_specs=(vmem,) * 3,
        scratch_shapes=[
            slots(C), slots(C), slots(C), slots(R), slots(R), slots(), slots(R), slots(C),
            slots(X), slots(X), slots(3, X), slots(3, X),
        ] + [dma((2, C)), dma((C,))] * 4 + [dma((X,)), dma((R,)), dma((R,))] * 3 + [
            dma((X,)), dma((3, X)), dma((X,)), dma((3, X)), dma((3,)), dma((3,)),
        ],
        compiler_params=pltpu.CompilerParams(
            collective_id=0, has_side_effects=True, vmem_limit_bytes=60 * 2**20),
    )(root_inverse, panel, node_inverse, mask)


def solution(mesh):
    placed = (
        P(("grp", "row"), "col"),
        P(("grp", "row"), "col"),
        P(("grp", "row"), "col"),
        P(("grp", "row")),
    )
    return jax.shard_map(
        functools.partial(shards, mesh.shape["row"], mesh.shape["col"]),
        mesh=mesh,
        in_specs=placed,
        out_specs=(P(("grp", "row"), "col"), P(("grp", "row"), "col"), P(("grp", "row"), "col")),
        check_vma=False,
    )
```

```python
import functools

import jax
import jax.numpy as jnp
from jax import lax
from jax.experimental import pallas as pl
from jax.experimental.pallas import tpu as pltpu
from jax.sharding import PartitionSpec as P

BS = 64
Q = 2
MESH = pl.DeviceIdType.MESH
F32, BF16 = jnp.float32, jnp.bfloat16


def halves(v):
    high = v.astype(BF16)
    return high, (v - high.astype(F32)).astype(BF16)


def multiply(dst, a, b, transposed, add):
    order = dst.shape[1]
    tile = min(256, order)
    dims = (((0 if transposed else 1,), (0,)), ((), ()))

    def dot(u, v):
        return lax.dot_general(u, v, dims, preferred_element_type=F32)

    def body(t, carry):
        cols = pl.ds(pl.multiple_of(t * tile, tile), tile)
        ah, al = halves(a[...])
        bh, bl = halves(b[:, cols])
        r = dot(ah, bh) + (dot(ah, bl) + dot(al, bh))
        if add:
            r = dst[:, cols] + r
        dst[:, cols] = r
        return carry

    lax.fori_loop(0, order // tile, body, 0)


def kernel(R, C, root, panel, node, mask, out_rr, out_or, out_nn,
           Mb, Rb, Nr, Nc, N0, X0, Xc, Yb, S, A, T1, T2,
           m_s, m_r, r_s, r_r, n_s, n_r, y_s, y_r,
           c_x, c_p, c_r, d_x, d_p, d_r, x_x, x_p, x_r, s1, q1, s2, q2, h_s, h_r):
    X = R // 2
    i, j = lax.axis_index("row"), lax.axis_index("col")
    x, c = i // 2, lax.rem(i, 2)
    mate = 2 * x + 1 - c
    left, right = lax.rem(j + C - 1, C), lax.rem(j + 1, C)
    k = R - 1 - i

    def copy(src, dst, ssem, rsem, row=None, col=None):
        device = {"row": i if row is None else row, "col": j if col is None else col}
        return pltpu.make_async_remote_copy(
            src_ref=src, dst_ref=dst, send_sem=ssem, recv_sem=rsem,
            device_id=device, device_id_type=MESH)

    def loop(low, high, body):
        def step(t, carry):
            body(t)
            return carry
        lax.fori_loop(low, high, step, 0)

    def when(*conditions):
        both = conditions[0]
        for condition in conditions[1:]:
            both = jnp.logical_and(both, condition)
        return pl.when(both)

    barrier = pltpu.get_barrier_semaphore()

    def greet(row, col):
        pl.semaphore_signal(barrier, inc=1, device_id={"row": row, "col": col}, device_id_type=MESH)

    @pl.when(j > 0)
    def _():
        greet(i, j - 1)

    @pl.when(j < C - 1)
    def _():
        greet(i, j + 1)

    greet(mate, j)
    loop(1, X, lambda d: greet(2 * lax.rem(x + d, X) + c, j))
    pl.semaphore_wait(barrier, X + jnp.where(j > 0, 1, 0) + jnp.where(j < C - 1, 1, 0))

    H = root.shape[0] // Q

    def rows(q):
        return pl.ds(q * H, H)

    def part(buf, l, q):
        return buf.at[l] if q is None else buf.at[l, rows(q)]

    def to_left(buf, sends, arrivals, l, q=None):
        ref, n = part(buf, l, q), l + C * (q or 0)
        return copy(ref, ref, sends.at[0, n], arrivals.at[n], col=left)

    def to_right(buf, sends, arrivals, l):
        return copy(buf.at[l], buf.at[l], sends.at[1, l], arrivals.at[l], col=right)

    def pass_on(buf, sends, arrivals, r, top, end, go_right, low=0, q=None):
        l = j + r

        @when(l <= top, l < C, j <= end, j >= low)
        def _():
            if not (isinstance(r, int) and r == 0):
                to_left(buf, sends, arrivals, l, q).wait_recv()

            @pl.when(j > low)
            def _():
                to_left(buf, sends, arrivals, l, q).start()

        if go_right:
            m = j - r

            @when(m >= 0, m <= top, j <= end)
            def _():
                if not (isinstance(r, int) and r == 0):
                    to_left(buf, sends, arrivals, m).wait_recv()

                @when(j < C - 1, j < end)
                def _():
                    to_right(buf, sends, arrivals, m).start()

    def sent_on(buf, sends, arrivals, top, end, go_right, low=0, q=None):
        def body(r):
            l, m = j + r, j - r

            @when(l <= top, l < C, j <= end, j > low)
            def _():
                to_left(buf, sends, arrivals, l, q).wait_send()

            if go_right:
                @when(m >= 0, m <= top, j <= end, j < C - 1, j < end)
                def _():
                    to_right(buf, sends, arrivals, m).wait_send()
        loop(0, C, body)

    def across(buf, sems, arrivals, d_chip, q):
        ref, n = part(buf, i, q), q or 0
        return copy(ref, ref, sems.at[d_chip + X * n], arrivals.at[i + R * n], row=2 * d_chip + c)

    def over(buf, sems, arrivals, l, q):
        ref, n = part(buf, l, q), l + R * (q or 0)
        return copy(ref, ref, sems.at[n], arrivals.at[n], row=mate)

    def spread(buf, xs, ps, arrivals, cross, own, q=None):
        def body(d):
            chip = lax.rem(x + d, X)

            @pl.when(cross(i, x, chip))
            def _():
                across(buf, xs, arrivals, chip, q).start()
        loop(1, X, body)

        @pl.when(own(i))
        def _():
            over(buf, ps, arrivals, i, q).start()

    def collect(buf, xs, ps, arrivals, cross, own, q=None):
        def body(d):
            chip = lax.rem(x + X - d, X)
            l = 2 * chip + c

            @pl.when(cross(l, chip, x))
            def _():
                over(buf, ps, arrivals, l, q).wait_recv()
                over(buf, ps, arrivals, l, q).start()
        loop(1, X, body)

        def rest(d):
            chip = lax.rem(x + X - d, X)
            l = 2 * chip + 1 - c

            @pl.when(jnp.where(chip == x, own(l), cross(l, chip, x)))
            def _():
                over(buf, ps, arrivals, l, q).wait_recv()
        loop(0, X, rest)

    def spread_done(buf, xs, ps, arrivals, cross, own, q=None):
        def body(d):
            chip = lax.rem(x + d, X)

            @pl.when(cross(i, x, chip))
            def _():
                across(buf, xs, arrivals, chip, q).wait_send()
            source = lax.rem(x + X - d, X)
            l = 2 * source + c

            @pl.when(cross(l, source, x))
            def _():
                over(buf, ps, arrivals, l, q).wait_send()
        loop(1, X, body)

        @pl.when(own(i))
        def _():
            over(buf, ps, arrivals, i, q).wait_send()

    def core_copy(n, chip):
        return copy(S.at[chip], T1.at[n, chip], s1.at[chip], q1.at[n, chip], row=mate)

    def chip_copy(n, chip, slot):
        return copy(A.at[chip], T2.at[n, slot], s2.at[chip], q2.at[n, slot], row=2 * chip + c)

    def sum_first(n, partial, into):
        def body(d):
            chip = lax.rem(x + d, X)

            @pl.when(into(x, chip))
            def _():
                partial(S.at[chip], 2 * chip + 1 - c)
                core_copy(n, chip).start()
                partial(A.at[chip], 2 * chip + c)
        loop(1, X + 1, body)

    def sum_second(n, into):
        def body(d):
            chip = lax.rem(x + d, X)

            @pl.when(into(x, chip))
            def _():
                core_copy(n, chip).wait_recv()
                A[chip] = A[chip] + T1[n, chip]

                @pl.when(chip != x)
                def _():
                    chip_copy(n, chip, x).start()
        loop(1, X + 1, body)

    def sum_last(n, out, into, sign):
        total = A.at[x]

        def body(d):
            chip = lax.rem(x + d, X)

            @pl.when(into(chip, x))
            def _():
                chip_copy(n, chip, chip).wait_recv()
                total[...] = total[...] + T2[n, chip]
        loop(1, X, body)
        out[...] = total[...] if sign > 0 else 0.0 - total[...]

        def sent(d):
            chip = lax.rem(x + d, X)

            @pl.when(into(x, chip))
            def _():
                core_copy(n, chip).wait_send()

                @pl.when(chip != x)
                def _():
                    chip_copy(n, chip, x).wait_send()
        loop(1, X + 1, sent)

    every = C - 1
    M_line = (Mb, m_s, m_r)
    R_line = (Rb, r_s, r_r)
    N_line = (Nr, n_s, n_r)
    Y_line = (Yb, y_s, y_r)
    N_col = (Nc, c_x, c_p, c_r, lambda l, a, b: l >= j, lambda l: l >= j)
    N0_col = (N0, d_x, d_p, d_r, lambda l, a, b: l >= 0, lambda l: l >= 0)
    X_col = (Xc, x_x, x_p, x_r, lambda l, a, b: a < b, lambda l: lax.rem(l, 2) == 0)

    def node_hop():
        return copy(Nc.at[i], N0.at[i], h_s.at[0], h_r.at[0], col=right)

    def panel_hop(q):
        return copy(part(Mb, 0, q), part(Mb, 0, q), h_s.at[1 + q], h_r.at[1 + q], col=right)

    def scaled_hop(q):
        n = 1 + Q + q
        return copy(X0.at[rows(q)], part(Xc, i, q), h_s.at[n], h_r.at[n], col=left)

    Nc[i] = node[...]

    @pl.when(j == 0)
    def _():
        node_hop().start()
    Mb[j] = panel[...] * mask[...]
    for q in range(Q):
        @pl.when(j == 0)
        def _():
            panel_hop(q).start()
        pass_on(*M_line, 0, every, every, False, 1, q)
    spread(*N_col)

    @when(c == 0, j != i + 1)
    def _():
        Rb[i + 1] = jnp.zeros(root.shape, F32)
    Rb[j] = root[...]
    pass_on(*R_line, 0, i, every, True)
    collect(*N_col)

    @pl.when(j == 1)
    def _():
        node_hop().wait_recv()
        spread(*N0_col)

    def scaled_part(dst, blocks, low, q):
        multiply(dst, part(Mb, low, q), blocks.at[low], False, False)
        loop(low + 1, C, lambda l: multiply(dst, part(Mb, l, q), blocks.at[l], False, True))

    for q in range(Q):
        loop(1, C, lambda r: pass_on(*M_line, r, every, every, False, 1, q))

        @pl.when(j == 1)
        def _():
            if q == 0:
                collect(*N0_col)
            panel_hop(q).wait_recv()
            scaled_part(X0.at[rows(q)], N0, 0, q)
            scaled_hop(q).start()

        @pl.when(j > 0)
        def _():
            scaled_part(part(Xc, i, q), Nc, j, q)
            spread(*X_col, q)
        if q == 0:
            pass_on(*R_line, 1, i, every, True)

            @pl.when(j <= k)
            def _():
                Nr[j] = Nc[k]
            pass_on(*N_line, 0, k, k, True)

    for q in range(Q):
        @pl.when(j == 0)
        def _():
            scaled_hop(q).wait_recv()
            spread(*X_col, q)

    def arrive(r):
        @pl.when(r > 1)
        def _():
            pass_on(*R_line, r, i, every, True)
        pass_on(*N_line, r, k, k, True)
    loop(1, C, arrive)

    for q in range(Q):
        collect(*X_col, q)

    multiply(Yb.at[j], Rb.at[0], Xc.at[0], False, False)
    loop(1, i + 1, lambda t: multiply(Yb.at[j], Rb.at[t], Xc.at[t], False, True))
    pass_on(*Y_line, 0, every, every, True)

    below = lambda a, b: b <= a
    sum_first(0, lambda dst, t: multiply(dst, Rb.at[t], Rb.at[j], True, False), below)
    sum_second(0, below)
    loop(1, C // 2, lambda r: pass_on(*Y_line, r, every, every, True))
    sum_last(0, out_rr, below, 1)

    sum_first(1, lambda dst, t: multiply(dst, Rb.at[t], Yb.at[j], True, False), below)
    sum_second(1, below)
    loop(C // 2, C, lambda r: pass_on(*Y_line, r, every, every, True))
    sum_last(1, out_or, below, -1)

    def node_part(dst, t):
        multiply(dst, Yb.at[t], Yb.at[j], True, False)

        @when(t <= k, j <= k)
        def _():
            multiply(dst, Nr.at[t], Nr.at[j], True, True)
    always = lambda a, b: a >= 0
    sum_first(2, node_part, always)
    sum_second(2, always)
    sum_last(2, out_nn, always, 1)

    for q in range(Q):
        sent_on(*M_line, every, every, False, 1, q)
        spread_done(*X_col, q)

    @pl.when(j == 0)
    def _():
        node_hop().wait_send()
        for q in range(Q):
            panel_hop(q).wait_send()

    @pl.when(j == 1)
    def _():
        for q in range(Q):
            scaled_hop(q).wait_send()
        spread_done(*N0_col)
    sent_on(*R_line, i, every, True)
    sent_on(*N_line, k, k, True)
    sent_on(*Y_line, every, every, True)
    spread_done(*N_col)


def shards(R, C, root_inverse, panel, node_inverse, structure):
    B = root_inverse.shape[0]
    X = R // 2
    mask = jnp.repeat(structure, BS).astype(F32)[:, None]
    block = jax.ShapeDtypeStruct((B, B), F32)
    dma = pltpu.SemaphoreType.DMA
    slots = lambda *n: pltpu.VMEM(n + (B, B), F32)
    vmem = pl.BlockSpec(memory_space=pltpu.VMEM)
    return pl.pallas_call(
        functools.partial(kernel, R, C),
        out_shape=(block, block, block),
        in_specs=[vmem] * 4,
        out_specs=(vmem,) * 3,
        scratch_shapes=[
            slots(C), slots(C), slots(C), slots(R), slots(R), slots(), slots(R), slots(C),
            slots(X), slots(X), slots(3, X), slots(3, X),
        ] + [dma((2, Q * C)), dma((Q * C,))] * 4 + [dma((Q * X,)), dma((Q * R,)), dma((Q * R,))] * 3 + [
            dma((X,)), dma((3, X)), dma((X,)), dma((3, X)), dma((1 + 2 * Q,)), dma((1 + 2 * Q,)),
        ],
        compiler_params=pltpu.CompilerParams(
            collective_id=0, has_side_effects=True, vmem_limit_bytes=60 * 2**20),
    )(root_inverse, panel, node_inverse, mask)


def solution(mesh):
    placed = (
        P(("grp", "row"), "col"),
        P(("grp", "row"), "col"),
        P(("grp", "row"), "col"),
        P(("grp", "row")),
    )
    return jax.shard_map(
        functools.partial(shards, mesh.shape["row"], mesh.shape["col"]),
        mesh=mesh,
        in_specs=placed,
        out_specs=(P(("grp", "row"), "col"), P(("grp", "row"), "col"), P(("grp", "row"), "col")),
        check_vma=False,
    )
```

```python
import functools

import jax
import jax.numpy as jnp
from jax import lax
from jax.experimental import pallas as pl
from jax.experimental.pallas import tpu as pltpu
from jax.sharding import PartitionSpec as P

BS = 64
Q = 2
MESH = pl.DeviceIdType.MESH
F32, BF16 = jnp.float32, jnp.bfloat16


def halves(v):
    high = v.astype(BF16)
    return high, (v - high.astype(F32)).astype(BF16)


def multiply(dst, a, b, transposed, add):
    order = dst.shape[1]
    tile = min(256, order)
    dims = (((0 if transposed else 1,), (0,)), ((), ()))

    def dot(u, v):
        return lax.dot_general(u, v, dims, preferred_element_type=F32)

    def body(t, carry):
        cols = pl.ds(pl.multiple_of(t * tile, tile), tile)
        ah, al = halves(a[...])
        bh, bl = halves(b[:, cols])
        r = dot(ah, bh) + (dot(ah, bl) + dot(al, bh))
        if add:
            r = dst[:, cols] + r
        dst[:, cols] = r
        return carry

    lax.fori_loop(0, order // tile, body, 0)


def kernel(R, C, root, panel, node, mask, out_rr, out_or, out_nn,
           Mb, Rb, Nr, Nc, N0, X0, Xc, Yb, S, A, T1, T2,
           m_s, m_r, r_s, r_r, n_s, n_r, y_s, y_r,
           c_x, c_p, c_r, d_x, d_p, d_r, x_x, x_p, x_r, s1, q1, s2, q2, h_s, h_r):
    X = R // 2
    i, j = lax.axis_index("row"), lax.axis_index("col")
    x, c = i // 2, lax.rem(i, 2)
    mate = 2 * x + 1 - c
    left, right = lax.rem(j + C - 1, C), lax.rem(j + 1, C)
    k = R - 1 - i

    def copy(src, dst, ssem, rsem, row=None, col=None):
        device = {"row": i if row is None else row, "col": j if col is None else col}
        return pltpu.make_async_remote_copy(
            src_ref=src, dst_ref=dst, send_sem=ssem, recv_sem=rsem,
            device_id=device, device_id_type=MESH)

    def loop(low, high, body):
        def step(t, carry):
            body(t)
            return carry
        lax.fori_loop(low, high, step, 0)

    def when(*conditions):
        both = conditions[0]
        for condition in conditions[1:]:
            both = jnp.logical_and(both, condition)
        return pl.when(both)

    barrier = pltpu.get_barrier_semaphore()

    def greet(row, col):
        pl.semaphore_signal(barrier, inc=1, device_id={"row": row, "col": col}, device_id_type=MESH)

    @pl.when(j > 0)
    def _():
        greet(i, j - 1)

    @pl.when(j < C - 1)
    def _():
        greet(i, j + 1)

    greet(mate, j)
    loop(1, X, lambda d: greet(2 * lax.rem(x + d, X) + c, j))
    pl.semaphore_wait(barrier, X + jnp.where(j > 0, 1, 0) + jnp.where(j < C - 1, 1, 0))

    H = root.shape[0] // Q

    def rows(q):
        return pl.ds(q * H, H)

    def part(buf, l, q):
        return buf.at[l] if q is None else buf.at[l, rows(q)]

    def to_left(buf, sends, arrivals, l, q=None):
        ref, n = part(buf, l, q), l + C * (q or 0)
        return copy(ref, ref, sends.at[0, n], arrivals.at[n], col=left)

    def to_right(buf, sends, arrivals, l):
        return copy(buf.at[l], buf.at[l], sends.at[1, l], arrivals.at[l], col=right)

    def pass_on(buf, sends, arrivals, r, top, end, go_right, low=0, q=None):
        l = j + r

        @when(l <= top, l < C, j <= end, j >= low)
        def _():
            if not (isinstance(r, int) and r == 0):
                to_left(buf, sends, arrivals, l, q).wait_recv()

            @pl.when(j > low)
            def _():
                to_left(buf, sends, arrivals, l, q).start()

        if go_right:
            m = j - r

            @when(m >= 0, m <= top, j <= end)
            def _():
                if not (isinstance(r, int) and r == 0):
                    to_left(buf, sends, arrivals, m).wait_recv()

                @when(j < C - 1, j < end)
                def _():
                    to_right(buf, sends, arrivals, m).start()

    def sent_on(buf, sends, arrivals, top, end, go_right, low=0, q=None):
        def body(r):
            l, m = j + r, j - r

            @when(l <= top, l < C, j <= end, j > low)
            def _():
                to_left(buf, sends, arrivals, l, q).wait_send()

            if go_right:
                @when(m >= 0, m <= top, j <= end, j < C - 1, j < end)
                def _():
                    to_right(buf, sends, arrivals, m).wait_send()
        loop(0, C, body)

    def across(buf, sems, arrivals, d_chip, q):
        ref, n = part(buf, i, q), q or 0
        return copy(ref, ref, sems.at[d_chip + X * n], arrivals.at[i + R * n], row=2 * d_chip + c)

    def over(buf, sems, arrivals, l, q):
        ref, n = part(buf, l, q), l + R * (q or 0)
        return copy(ref, ref, sems.at[n], arrivals.at[n], row=mate)

    def spread(buf, xs, ps, arrivals, cross, own, q=None):
        def body(d):
            chip = lax.rem(x + d, X)

            @pl.when(cross(i, x, chip))
            def _():
                across(buf, xs, arrivals, chip, q).start()
        loop(1, X, body)

        @pl.when(own(i))
        def _():
            over(buf, ps, arrivals, i, q).start()

    def collect(buf, xs, ps, arrivals, cross, own, q=None):
        def body(d):
            chip = lax.rem(x + X - d, X)
            l = 2 * chip + c

            @pl.when(cross(l, chip, x))
            def _():
                over(buf, ps, arrivals, l, q).wait_recv()
                over(buf, ps, arrivals, l, q).start()
        loop(1, X, body)

        def rest(d):
            chip = lax.rem(x + X - d, X)
            l = 2 * chip + 1 - c

            @pl.when(jnp.where(chip == x, own(l), cross(l, chip, x)))
            def _():
                over(buf, ps, arrivals, l, q).wait_recv()
        loop(0, X, rest)

    def spread_done(buf, xs, ps, arrivals, cross, own, q=None):
        def body(d):
            chip = lax.rem(x + d, X)

            @pl.when(cross(i, x, chip))
            def _():
                across(buf, xs, arrivals, chip, q).wait_send()
            source = lax.rem(x + X - d, X)
            l = 2 * source + c

            @pl.when(cross(l, source, x))
            def _():
                over(buf, ps, arrivals, l, q).wait_send()
        loop(1, X, body)

        @pl.when(own(i))
        def _():
            over(buf, ps, arrivals, i, q).wait_send()

    def core_copy(n, chip):
        return copy(S.at[chip], T1.at[n, chip], s1.at[chip], q1.at[n, chip], row=mate)

    def chip_copy(n, chip, slot):
        return copy(A.at[chip], T2.at[n, slot], s2.at[chip], q2.at[n, slot], row=2 * chip + c)

    def sum_first(n, partial, into):
        def body(d):
            chip = lax.rem(x + d, X)

            @pl.when(into(x, chip))
            def _():
                partial(S.at[chip], 2 * chip + 1 - c)
                core_copy(n, chip).start()
                partial(A.at[chip], 2 * chip + c)
        loop(1, X + 1, body)

    def sum_second(n, into):
        def body(d):
            chip = lax.rem(x + d, X)

            @pl.when(into(x, chip))
            def _():
                core_copy(n, chip).wait_recv()
                A[chip] = A[chip] + T1[n, chip]

                @pl.when(chip != x)
                def _():
                    chip_copy(n, chip, x).start()
        loop(1, X + 1, body)

    def sum_last(n, out, into, sign):
        total = A.at[x]

        def body(d):
            chip = lax.rem(x + d, X)

            @pl.when(into(chip, x))
            def _():
                chip_copy(n, chip, chip).wait_recv()
                total[...] = total[...] + T2[n, chip]
        loop(1, X, body)
        out[...] = total[...] if sign > 0 else 0.0 - total[...]

        def sent(d):
            chip = lax.rem(x + d, X)

            @pl.when(into(x, chip))
            def _():
                core_copy(n, chip).wait_send()

                @pl.when(chip != x)
                def _():
                    chip_copy(n, chip, x).wait_send()
        loop(1, X + 1, sent)

    every = C - 1
    M_line = (Mb, m_s, m_r)
    R_line = (Rb, r_s, r_r)
    N_line = (Nr, n_s, n_r)
    Y_line = (Yb, y_s, y_r)
    N_col = (Nc, c_x, c_p, c_r, lambda l, a, b: l >= j, lambda l: l >= j)
    N0_col = (N0, d_x, d_p, d_r, lambda l, a, b: l >= 0, lambda l: l >= 0)
    X_col = (Xc, x_x, x_p, x_r, lambda l, a, b: a < b, lambda l: lax.rem(l, 2) == 0)

    def node_hop():
        return copy(Nc.at[i], N0.at[i], h_s.at[0], h_r.at[0], col=right)

    def panel_hop(q):
        return copy(part(Mb, 0, q), part(Mb, 0, q), h_s.at[1 + q], h_r.at[1 + q], col=right)

    def scaled_hop(q):
        n = 1 + Q + q
        return copy(X0.at[rows(q)], part(Xc, i, q), h_s.at[n], h_r.at[n], col=left)

    Nc[i] = node[...]

    @pl.when(j == 0)
    def _():
        node_hop().start()
    Mb[j] = panel[...] * mask[...]
    for q in range(Q):
        @pl.when(j == 0)
        def _():
            panel_hop(q).start()
        pass_on(*M_line, 0, every, every, False, 1, q)
    spread(*N_col)

    @when(c == 0, j != i + 1)
    def _():
        Rb[i + 1] = jnp.zeros(root.shape, F32)
    Rb[j] = root[...]
    pass_on(*R_line, 0, i, every, True)
    collect(*N_col)

    @pl.when(j == 1)
    def _():
        node_hop().wait_recv()
        spread(*N0_col)

    def scaled_part(dst, blocks, low, q):
        multiply(dst, part(Mb, low, q), blocks.at[low], False, False)
        loop(low + 1, C, lambda l: multiply(dst, part(Mb, l, q), blocks.at[l], False, True))

    for q in range(Q):
        loop(1, C, lambda r: pass_on(*M_line, r, every, every, False, 1, q))

        @pl.when(j == 1)
        def _():
            if q == 0:
                collect(*N0_col)
            panel_hop(q).wait_recv()
            scaled_part(X0.at[rows(q)], N0, 0, q)
            scaled_hop(q).start()

        @pl.when(j > 0)
        def _():
            scaled_part(part(Xc, i, q), Nc, j, q)
            spread(*X_col, q)
        if q == 0:
            pass_on(*R_line, 1, i, every, True)

            @pl.when(j <= k)
            def _():
                Nr[j] = Nc[k]
            pass_on(*N_line, 0, k, k, True)

    for q in range(Q):
        @pl.when(j == 0)
        def _():
            scaled_hop(q).wait_recv()
            spread(*X_col, q)

    loop(2, C, lambda r: pass_on(*R_line, r, i, every, True))

    for q in range(Q):
        collect(*X_col, q)

    multiply(Yb.at[j], Rb.at[0], Xc.at[0], False, False)
    loop(1, i + 1, lambda t: multiply(Yb.at[j], Rb.at[t], Xc.at[t], False, True))
    pass_on(*Y_line, 0, every, every, True)

    def arrive(r):
        pass_on(*N_line, r, k, k, True)
        pass_on(*Y_line, r, every, every, True)

    below = lambda a, b: b <= a
    sum_first(0, lambda dst, t: multiply(dst, Rb.at[t], Rb.at[j], True, False), below)
    sum_second(0, below)
    loop(1, C // 2, arrive)
    sum_last(0, out_rr, below, 1)

    sum_first(1, lambda dst, t: multiply(dst, Rb.at[t], Yb.at[j], True, False), below)
    sum_second(1, below)
    loop(C // 2, C, arrive)
    sum_last(1, out_or, below, -1)

    def node_part(dst, t):
        multiply(dst, Yb.at[t], Yb.at[j], True, False)

        @when(t <= k, j <= k)
        def _():
            multiply(dst, Nr.at[t], Nr.at[j], True, True)
    always = lambda a, b: a >= 0
    sum_first(2, node_part, always)
    sum_second(2, always)
    sum_last(2, out_nn, always, 1)

    for q in range(Q):
        sent_on(*M_line, every, every, False, 1, q)
        spread_done(*X_col, q)

    @pl.when(j == 0)
    def _():
        node_hop().wait_send()
        for q in range(Q):
            panel_hop(q).wait_send()

    @pl.when(j == 1)
    def _():
        for q in range(Q):
            scaled_hop(q).wait_send()
        spread_done(*N0_col)
    sent_on(*R_line, i, every, True)
    sent_on(*N_line, k, k, True)
    sent_on(*Y_line, every, every, True)
    spread_done(*N_col)


def shards(R, C, root_inverse, panel, node_inverse, structure):
    B = root_inverse.shape[0]
    X = R // 2
    mask = jnp.repeat(structure, BS).astype(F32)[:, None]
    block = jax.ShapeDtypeStruct((B, B), F32)
    dma = pltpu.SemaphoreType.DMA
    slots = lambda *n: pltpu.VMEM(n + (B, B), F32)
    vmem = pl.BlockSpec(memory_space=pltpu.VMEM)
    return pl.pallas_call(
        functools.partial(kernel, R, C),
        out_shape=(block, block, block),
        in_specs=[vmem] * 4,
        out_specs=(vmem,) * 3,
        scratch_shapes=[
            slots(C), slots(C), slots(C), slots(R), slots(R), slots(), slots(R), slots(C),
            slots(X), slots(X), slots(3, X), slots(3, X),
        ] + [dma((2, Q * C)), dma((Q * C,))] * 4 + [dma((Q * X,)), dma((Q * R,)), dma((Q * R,))] * 3 + [
            dma((X,)), dma((3, X)), dma((X,)), dma((3, X)), dma((1 + 2 * Q,)), dma((1 + 2 * Q,)),
        ],
        compiler_params=pltpu.CompilerParams(
            collective_id=0, has_side_effects=True, vmem_limit_bytes=60 * 2**20),
    )(root_inverse, panel, node_inverse, mask)


def solution(mesh):
    placed = (
        P(("grp", "row"), "col"),
        P(("grp", "row"), "col"),
        P(("grp", "row"), "col"),
        P(("grp", "row")),
    )
    return jax.shard_map(
        functools.partial(shards, mesh.shape["row"], mesh.shape["col"]),
        mesh=mesh,
        in_specs=placed,
        out_specs=(P(("grp", "row"), "col"), P(("grp", "row"), "col"), P(("grp", "row"), "col")),
        check_vma=False,
    )
```
